32 devices in a mesh: shard: 2 (over x), rep: 16 (over z, y, core).
Axes of the slice: x: 2, y: 2, z: 4, core: 2. Of those that a mesh axis runs over, the one named last changes fastest.
Arguments:
- tokens: bfloat16 [16384, 1024], P(('shard', 'rep')), may hold values from -6 to 6
- routes: int32 [16384, 8], P(('shard', 'rep')), may hold values from 0 to 15, all different within a row; in each aligned block of 512 rows (0 to 511, 512 to 1023, ...) at most 288 rows name the same one
- out_grad: bfloat16 [16384, 1024], P(('shard', 'rep')), may hold values from -6 to 6
- query_weight: bfloat16 [1024, 1024], P('shard'), may hold values from -0.625 to 0.625
- key_weight: bfloat16 [1024, 512], P('shard'), may hold values from -0.625 to 0.625
- value_weight: bfloat16 [1024, 512], P('shard'), may hold values from -0.1875 to 0.1875
- output_weight: bfloat16 [1024, 1024], P('shard'), may hold values from -4 to 4
- norm_one: bfloat16 [1024], P('shard'), may hold values from 0.5 to 1.5
- norm_two: bfloat16 [1024], P('shard'), may hold values from 0.5 to 1.5
- router_weight: bfloat16 [1024, 16], P('shard'), may hold values from -0.09375 to 0.09375
- expert_in: bfloat16 [16, 2, 1024, 512], P('shard'), may hold values from -0.1875 to 0.1875
- expert_out: bfloat16 [16, 1024, 512], P('shard'), may hold values from -4 to 4
Outputs:
- layer_out: bfloat16 [16384, 1024], P(('shard', 'rep'))
- tokens_grad: float32 [16384, 1024], P(('shard', 'rep'))
- query_grad: float32 [1024, 1024], P('shard')
- key_grad: float32 [1024, 512], P('shard')
- value_grad: float32 [1024, 512], P('shard')
- output_grad: float32 [1024, 1024], P('shard')
- norm_one_grad: float32 [1024], P('shard')
- norm_two_grad: float32 [1024], P('shard')
- router_grad: float32 [1024, 16], P('shard')
- expert_in_grad: float32 [16, 2, 1024, 512], P('shard')
- expert_out_grad: float32 [16, 1024, 512], P('shard')
The draws below stay inside these ranges and needn't reach their ends.
Inputs may be any that keep to these rules, and one draw needn't show every extreme that they name: `routes`: each row names 8 different experts. Among the 512 rows of one device no expert is named more than 288 times, and in every draw some expert is named exactly 288 times in some device's rows.
All inputs are finite; a program needn't handle non-finite values.
Results may differ from the reference program's by a relative error of at most 0.02.
Values may be sent and summed in bfloat16 or wider, within the bound.
A program may use at most 448 MiB of HBM per device.

```python
import math
import jax
import jax.numpy as jnp
import numpy as np
from jax import lax

D = 1024
HEADS = 16
KV_HEADS = 8
HEAD_DIM = 64
FF = 512
EXPERTS = 16
TOP = 8
SEQ = 512
TOK_DEV = 512
TOKENS = 16384
CAP = 288


def levels(own_key, extent, split, low, high):
    gain, own = 1.0, jax.random.fold_in(own_key, 6)
    for dim, blocks in split:
        draws = jnp.exp(jax.random.uniform(jax.random.fold_in(own, dim), (blocks,), jnp.float32, low / len(split), high / len(split)))
        gain = gain * jnp.repeat(draws, extent[dim] // blocks).reshape([-1 if axis == dim else 1 for axis in range(len(extent))])
    return gain


def routed_block(own_key, own, number, rows, number_of, top, limit, lean):
    sequence = jax.random.permutation(own_key, number_of)
    packed, ordinary = portions_of(number_of, rows * top, limit, lean, True), portions_of(number_of, rows * top, limit, lean, False)
    places = jnp.arange(number_of)

    def named(sizes, rotation):
        used = int((sizes > 0).sum())
        fixed = max(1, used // 4)
        shifted = fixed + (places - fixed + rotation * (used - fixed)) % max(1, number_of - fixed)
        return jnp.zeros((number_of,), jnp.int32).at[sequence[jnp.where(places < fixed, places, shifted)]].set(jnp.asarray(sizes, jnp.int32))

    sizes = jnp.where(number % 4 == 0, named(packed, number // 4), named(ordinary, number - number // 4 - 1))
    mixed = jax.random.permutation(jax.random.fold_in(own, 3), number_of)
    source_of, taker = mixed[0:number_of // 2 * 2:2], mixed[1:number_of // 2 * 2:2]
    margin = jnp.minimum(sizes[source_of] - 1, limit - sizes[taker]) // 2
    margin = jnp.where((source_of == sequence[0]) | (taker == sequence[0]) | (sizes[taker] == 0), 0, jnp.maximum(margin, 0))
    shifted = jax.random.randint(jax.random.fold_in(own, 4), (number_of // 2,), 0, 1 << 20) % (margin + 1)
    sizes = sizes.at[source_of].add(-shifted).at[taker].add(shifted)
    labels = jnp.searchsorted(jnp.cumsum(sizes), jnp.arange(rows * top), side="right").astype(jnp.int32)
    listing = labels.reshape(top, rows).T
    listing = listing[jax.random.permutation(jax.random.fold_in(own, 1), rows)]
    rotation = jax.random.randint(jax.random.fold_in(own, 2), (rows, 1), 0, top)
    return jnp.take_along_axis(listing, (jnp.arange(top)[None, :] + rotation) % top, axis=1)


def portions_of(count, total, bound, skew, full):
    weights = [(1 << 20) // math.isqrt(standing ** skew) + 1 for standing in range(1, count + 1)]
    largest = bound if full else min(bound, max(-(-total // count), total * weights[0] // sum(weights)))
    least = 1 if total - largest >= count - 1 else 0
    counts, rest = [largest] + [least] * (count - 1), total - largest - least * (count - 1)
    while rest > 0:
        candidates = [i for i in range(1, count) if counts[i] < largest] or [i for i in range(1, count) if counts[i] < bound]
        mass, remaining = sum([weights[i] for i in candidates]), rest
        for i in candidates:
            extra = min(bound - counts[i], max(1, remaining * weights[i] // mass), rest)
            counts[i] = counts[i] + extra
            rest = rest - extra
    return np.array(counts)


def bell_draw(key, extent, scale, most, shards=(), kind=jnp.bfloat16):
    level = levels(key, extent, shards, -0.22, 0.18) if shards else 1.0
    array = jax.random.normal(key, extent, jnp.float32) * scale * level
    return jnp.minimum(jnp.maximum(array, -most), most).astype(kind)


def setup_inputs(seed: int = 0) -> dict:
    arg_keys = jax.random.split(jax.random.key(seed), 13)
    tokens = bell_draw(arg_keys[0], (TOKENS, D), 1.0, 6.0, ((0, 32),))
    routes_keys = jax.random.split(jax.random.fold_in(arg_keys[1], 1), TOKENS // TOK_DEV)
    routes_turns = jax.random.permutation(jax.random.fold_in(arg_keys[1], 3), TOKENS // TOK_DEV)
    routes = jax.vmap(lambda own, number: routed_block(jax.random.fold_in(arg_keys[1], 2), own, number, TOK_DEV, EXPERTS, TOP, CAP, 1))(routes_keys, routes_turns).reshape((TOKENS, TOP))
    out_grad = bell_draw(arg_keys[2], (TOKENS, D), 1.0, 6.0, ((0, 32),))
    query_weight = bell_draw(arg_keys[3], (D, HEADS * HEAD_DIM), (D // 12) ** -0.5, 0.625, ((0, 2),))
    key_weight = bell_draw(arg_keys[4], (D, KV_HEADS * HEAD_DIM), (D // 12) ** -0.5, 0.625, ((0, 2),))
    value_weight = bell_draw(arg_keys[5], (D, KV_HEADS * HEAD_DIM), D ** -0.5, 0.1875, ((0, 2),))
    output_weight = bell_draw(arg_keys[6], (HEADS * HEAD_DIM, D), 2 ** -0.5, 4.0, ((0, 2),))
    norm_one = jnp.clip(1.0 + 0.1 * jax.random.normal(arg_keys[7], (D,), jnp.float32), 0.5, 1.5).astype(jnp.bfloat16)
    norm_two = jnp.clip(1.0 + 0.1 * jax.random.normal(arg_keys[8], (D,), jnp.float32), 0.5, 1.5).astype(jnp.bfloat16)
    router_weight = bell_draw(arg_keys[9], (D, EXPERTS), (4 * D) ** -0.5, 0.09375, ((0, 2),))
    expert_in = bell_draw(arg_keys[10], (EXPERTS, 2, D, FF), D ** -0.5, 0.1875, ((0, 2),))
    expert_out = bell_draw(arg_keys[11], (EXPERTS, D, FF), (max(FF // 256, 1)) ** -0.5, 4.0, ((0, 2),))
    return {"tokens": tokens, "routes": routes, "out_grad": out_grad, "query_weight": query_weight, "key_weight": key_weight, "value_weight": value_weight, "output_weight": output_weight, "norm_one": norm_one, "norm_two": norm_two, "router_weight": router_weight, "expert_in": expert_in, "expert_out": expert_out}


EPSILON = 1e-06
ATTN_SCALE = 0.015625
RESIDUAL_SCALE = 0.22
ROPE_BASE = 10000.0

@jax.custom_vjp
def low(v):
    return lax.optimization_barrier(v.astype(jnp.bfloat16)).astype(jnp.float32)

@jax.custom_vjp
def low_back(v):
    return v

def low_keep(v):
    return (low(v), None)

def low_pass(kept, grad):
    return (grad,)

def back_keep(v):
    return (v, None)

def back_low(kept, grad):
    return (low(grad),)
low.defvjp(low_keep, low_pass)
low_back.defvjp(back_keep, back_low)

def rope_tables(length, width):
    half_width = width // 2
    frequency = ROPE_BASE ** (-2.0 * jnp.arange(half_width, dtype=jnp.float32) / width)
    angles = jnp.arange(length, dtype=jnp.float32)[:, None] * frequency[None, :]
    return (jnp.cos(angles)[:, None, :], jnp.sin(angles)[:, None, :])

def rotate(values, cosine, sine_part):
    half_width = values.shape[-1] // 2
    first_half = values[..., :half_width]
    second_half = values[..., half_width:]
    return jnp.concatenate([first_half * cosine - second_half * sine_part, second_half * cosine + first_half * sine_part], -1)

def dispatch(routes):
    token_count = routes.shape[0]
    experts_iota = jnp.arange(EXPERTS, dtype=jnp.int32)
    onehot = (routes[:, :, None] == experts_iota[None, None, :]).astype(jnp.int32)
    chosen_any = lax.optimization_barrier(jnp.sum(onehot, 1)).astype(jnp.int32)
    slot_ranks = (jnp.cumsum(chosen_any, 0) - chosen_any).astype(jnp.int32)
    slot_place = lax.optimization_barrier(jnp.sum(onehot * slot_ranks[:, None, :], 2)).astype(jnp.int32)
    slot_of = (routes * CAP + slot_place).astype(jnp.int32)
    sources = jnp.broadcast_to(jnp.arange(token_count, dtype=jnp.int32)[:, None], routes.shape)
    token_of = jnp.full((EXPERTS * CAP,), token_count, jnp.int32).at[slot_of.reshape(-1)].set(sources.reshape(-1))
    return (onehot, slot_of, token_of)

def layer_group(weights, inputs_group, routes_group):
    query_weight, key_weight, value_weight, output_weight, norm_one, norm_two, router_weight, expert_in, expert_out = weights
    row_count = inputs_group.shape[0]
    seq_count = row_count // SEQ
    group_heads = HEADS // KV_HEADS
    exact = lax.Precision.HIGHEST
    scale_one = lax.rsqrt(lax.optimization_barrier(jnp.mean(inputs_group * inputs_group, -1, keepdims=True)) + EPSILON)
    normed_one = low(inputs_group * scale_one * norm_one)
    query_pre = low_back(jnp.dot(normed_one, query_weight, precision=exact))
    key_pre = low_back(jnp.dot(normed_one, key_weight, precision=exact))
    value_low = low(low_back(jnp.dot(normed_one, value_weight, precision=exact))).reshape(seq_count, SEQ, KV_HEADS, HEAD_DIM)
    cosine, sine_part = rope_tables(SEQ, HEAD_DIM)
    queries = low(rotate(query_pre.reshape(seq_count, SEQ, HEADS, HEAD_DIM), cosine, sine_part))
    queries = queries.reshape(seq_count, SEQ, KV_HEADS, group_heads, HEAD_DIM)
    keys_low = low(rotate(key_pre.reshape(seq_count, SEQ, KV_HEADS, HEAD_DIM), cosine, sine_part))
    scores = low_back(ATTN_SCALE * jnp.einsum('sqgjd,skgd->sgjqk', queries, keys_low, precision=exact))
    positions = jnp.arange(SEQ)
    scores = jnp.where(positions[:, None] >= positions[None, :], scores, -jnp.inf)
    probs_low = low(jax.nn.softmax(scores, -1))
    attended = jnp.einsum('sgjqk,skgd->sqgjd', probs_low, value_low, precision=exact).reshape(row_count, HEADS * HEAD_DIM)
    attended = low(low_back(attended))
    residual = inputs_group + RESIDUAL_SCALE * low_back(jnp.dot(attended, output_weight, precision=exact))
    scale_two = lax.rsqrt(lax.optimization_barrier(jnp.mean(residual * residual, -1, keepdims=True)) + EPSILON)
    normed_two = low(residual * scale_two * norm_two)
    onehot, slot_of, token_of = dispatch(routes_group)
    onehot_f = onehot.astype(jnp.float32)
    logits = jnp.dot(normed_two, router_weight, precision=exact)
    gate_weights = jax.nn.softmax(lax.optimization_barrier(jnp.sum(onehot_f * logits[:, None, :], -1)), -1)
    padded = jnp.concatenate([normed_two, jnp.zeros((1, D), jnp.float32)], 0)
    expert_rows = padded[token_of].reshape(EXPERTS, CAP, D)
    pre_act = low_back(jnp.einsum('ecd,etdf->tecf', expert_rows, expert_in, precision=exact))
    hidden = low(jax.nn.silu(pre_act[0]) * pre_act[1])
    slot_outputs = low_back(jnp.einsum('ecf,edf->ecd', hidden, expert_out, precision=exact)).reshape(EXPERTS * CAP, D)
    expert_mix = lax.optimization_barrier(jnp.sum(gate_weights[:, :, None] * slot_outputs[slot_of], 1))
    return residual + RESIDUAL_SCALE * expert_mix

def reference(tokens, routes, out_grad, query_weight, key_weight, value_weight, output_weight, norm_one, norm_two, router_weight, expert_in, expert_out):
    params = tuple((weight.astype(jnp.float32) for weight in (query_weight, key_weight, value_weight, output_weight, norm_one, norm_two, router_weight, expert_in, expert_out)))
    inputs_all = tokens.astype(jnp.float32).reshape(-1, TOK_DEV, D)
    route_groups = routes.reshape(-1, TOK_DEV, TOP)
    group_step = jax.checkpoint(layer_group)

    def forward(weights, inputs_given):

        def scan_step(carried, group_item):
            return (carried, group_step(weights, group_item[0], group_item[1]))
        return lax.scan(scan_step, jnp.zeros((), jnp.float32), (inputs_given, route_groups))[1]
    outputs, pullback = jax.vjp(forward, params, inputs_all)
    weight_grads, input_grads = pullback(out_grad.astype(jnp.float32).reshape(inputs_all.shape))
    layer_out = outputs.reshape(tokens.shape).astype(jnp.bfloat16)
    return (layer_out, input_grads.reshape(tokens.shape), weight_grads[0], weight_grads[1], weight_grads[2], weight_grads[3], weight_grads[4], weight_grads[5], weight_grads[6], weight_grads[7], weight_grads[8])
```

```python
import functools

import jax
import jax.numpy as jnp
from jax import lax
from jax.sharding import PartitionSpec as P

D = 1024
HEADS = 16
KV_HEADS = 8
HEAD_DIM = 64
EXPERTS = 16
SEQ = 512
CAP = 288


EPSILON = 1e-06
ATTN_SCALE = 0.015625
RESIDUAL_SCALE = 0.22
ROPE_BASE = 10000.0


def rope_tables(length, width):
    half_width = width // 2
    frequency = ROPE_BASE ** (-2.0 * jnp.arange(half_width, dtype=jnp.float32) / width)
    angles = jnp.arange(length, dtype=jnp.float32)[:, None] * frequency[None, :]
    return (jnp.cos(angles)[:, None, :], jnp.sin(angles)[:, None, :])


def rotate(values, cosine, sine_part):
    half_width = values.shape[-1] // 2
    first_half = values[..., :half_width]
    second_half = values[..., half_width:]
    return jnp.concatenate(
        [
            first_half * cosine - second_half * sine_part,
            second_half * cosine + first_half * sine_part,
        ],
        -1,
    )


def unrotate(values, cosine, sine_part):
    half_width = values.shape[-1] // 2
    first_half = values[..., :half_width]
    second_half = values[..., half_width:]
    return jnp.concatenate(
        [
            first_half * cosine + second_half * sine_part,
            second_half * cosine - first_half * sine_part,
        ],
        -1,
    )


def block_scores(query_block, key_block, first_row):
    scores = ATTN_SCALE * jnp.einsum(
        "sqgjd,skgd->sgjqk", query_block, key_block, preferred_element_type=jnp.float32
    )
    query_pos = first_row + jnp.arange(query_block.shape[1])
    key_pos = jnp.arange(key_block.shape[1])
    return jnp.where(query_pos[:, None] >= key_pos[None, :], scores, -jnp.inf)


def shift(value, axis, size, step):
    return lax.ppermute(value, axis, [(i, (i + step) % size) for i in range(size)])


def after(value, *others):
    return lax.optimization_barrier((value,) + others)[0]


def gather_rows(block, shards, reps):
    me = lax.axis_index("shard")
    odd = lax.rem(lax.axis_index("rep"), 2)
    rows, width = block.shape
    half = rows // 2
    mine = lax.dynamic_slice_in_dim(block, odd * half, half, 0)
    swap = [(i, i ^ 1) for i in range(reps)]
    whole = jnp.zeros((shards * rows, width), block.dtype)
    whole = lax.dynamic_update_slice_in_dim(whole, block, me * rows, 0)
    for step in range(1, shards):
        owner = lax.rem(me - step + shards, shards)
        first = shift(mine, "shard", shards, step)
        second = lax.ppermute(first, "rep", swap)
        whole = lax.dynamic_update_slice_in_dim(whole, first, owner * rows + odd * half, 0)
        whole = lax.dynamic_update_slice_in_dim(whole, second, owner * rows + (1 - odd) * half, 0)
    return whole


def per_device(
    shards,
    reps,
    tokens,
    routes,
    out_grad,
    query_weight,
    key_weight,
    value_weight,
    output_weight,
    norm_one,
    norm_two,
    router_weight,
    expert_in,
    expert_out,
):
    row_count = tokens.shape[0]
    seq_count = row_count // SEQ
    group_heads = HEADS // KV_HEADS
    query_width = HEADS * HEAD_DIM
    kv_width = KV_HEADS * HEAD_DIM
    local = EXPERTS // shards
    low = jnp.bfloat16
    me = lax.axis_index("shard")
    side = jnp.concatenate(
        [router_weight, norm_one[:, None], norm_two[:, None]]
        + [jnp.zeros((router_weight.shape[0], 128 - EXPERTS - 2), low)],
        1,
    )
    first_full = gather_rows(
        jnp.concatenate([query_weight, key_weight, value_weight, side], 1), shards, reps
    )
    output_full = gather_rows(after(output_weight, first_full), shards, reps)
    qkv_full = first_full[:, : query_width + 2 * kv_width]
    query_full = first_full[:, :query_width]
    key_full = first_full[:, query_width : query_width + kv_width]
    value_full = first_full[:, query_width + kv_width : query_width + 2 * kv_width]
    base = query_width + 2 * kv_width
    router_full = first_full[:, base : base + EXPERTS]
    gain_one = first_full[:, base + EXPERTS].astype(jnp.float32)
    gain_two = first_full[:, base + EXPERTS + 1].astype(jnp.float32)
    grad_send = after(out_grad, output_full)
    grad_groups = [out_grad] + [shift(grad_send, "shard", shards, k) for k in range(1, shards)]
    route_groups = [routes] + [shift(routes, "shard", shards, k) for k in range(1, shards)]

    inputs_f = tokens.astype(jnp.float32)
    scale_one = lax.rsqrt(jnp.mean(inputs_f * inputs_f, -1, keepdims=True) + EPSILON)
    normed_one = (inputs_f * scale_one * gain_one).astype(low)
    query_pre = jnp.dot(normed_one, query_full, preferred_element_type=jnp.float32)
    key_pre = jnp.dot(normed_one, key_full, preferred_element_type=jnp.float32)
    value_low = jnp.dot(normed_one, value_full, preferred_element_type=jnp.float32).astype(low)
    value_low = value_low.reshape(seq_count, SEQ, KV_HEADS, HEAD_DIM)
    cosine, sine_part = rope_tables(SEQ, HEAD_DIM)
    queries = rotate(query_pre.reshape(seq_count, SEQ, HEADS, HEAD_DIM), cosine, sine_part).astype(
        low
    )
    queries = queries.reshape(seq_count, SEQ, KV_HEADS, group_heads, HEAD_DIM)
    keys_low = rotate(
        key_pre.reshape(seq_count, SEQ, KV_HEADS, HEAD_DIM), cosine, sine_part
    ).astype(low)
    scores = block_scores(queries, keys_low, 0)
    row_max = jnp.max(scores, -1, keepdims=True)
    exp_scores = jnp.exp(scores - row_max)
    row_total = jnp.sum(exp_scores, -1, keepdims=True)
    prob_low = (exp_scores / row_total).astype(low)
    head_outputs = jnp.einsum(
        "sgjqk,skgd->sqgjd", prob_low, value_low, preferred_element_type=jnp.float32
    )
    log_total = row_max + jnp.log(row_total)
    attended = head_outputs.reshape(row_count, query_width).astype(low)
    branch = jnp.dot(attended, output_full, preferred_element_type=jnp.float32)
    residual = inputs_f + RESIDUAL_SCALE * branch
    scale_two = lax.rsqrt(jnp.mean(residual * residual, -1, keepdims=True) + EPSILON)
    normed_two = (residual * scale_two * gain_two).astype(low)

    group_rows = [normed_two] + [shift(normed_two, "shard", shards, k) for k in range(1, shards)]
    experts_iota = jnp.arange(EXPERTS, dtype=jnp.int32)
    triangle = (jnp.arange(row_count)[:, None] > jnp.arange(row_count)[None, :]).astype(low)

    def gates_of(rows, group_routes):
        named = jnp.any(group_routes[:, :, None] == experts_iota, 1)
        logits = jnp.dot(rows, router_full, preferred_element_type=jnp.float32)
        return named, jax.nn.softmax(jnp.where(named, logits, -jnp.inf), -1)

    def mine_of(table):
        return lax.dynamic_slice_in_dim(table, me * local, local, 1)

    spreads, rows_slots, grad_slots, gate_slots = [], [], [], []
    slots = jnp.arange(CAP, dtype=jnp.int32)
    home = None
    for k in range(shards):
        named, gates = gates_of(group_rows[k], route_groups[k])
        if k == 0:
            home = (named, gates)
        ranks = jnp.dot(triangle, named.astype(low), preferred_element_type=jnp.float32)
        ranks = jnp.where(named, ranks.astype(jnp.int32), -1)
        place = mine_of(ranks).T
        hit = place[:, None, :] == slots[None, :, None]
        spread = hit.astype(low)
        spreads.append(spread)
        flat = spread.reshape(local * CAP, row_count)
        rows_slots.append(
            jnp.dot(flat, group_rows[k], preferred_element_type=jnp.float32)
            .astype(low)
            .reshape(local, CAP, D)
        )
        grad_slots.append(
            jnp.dot(flat, grad_groups[k], preferred_element_type=jnp.float32)
            .astype(low)
            .reshape(local, CAP, D)
        )
        gate_slots.append(jnp.sum(jnp.where(hit, mine_of(gates).T[:, None, :], 0.0), -1))
    rows_in = jnp.concatenate(rows_slots, 1)
    grads_in = jnp.concatenate(grad_slots, 1)
    slot_gate = jnp.concatenate(gate_slots, 1)[:, :, None] * RESIDUAL_SCALE

    def up(part):
        return jnp.einsum(
            "ecd,edf->ecf", rows_in, expert_in[:, part], preferred_element_type=jnp.float32
        )

    gate_act, up_act = up(0), up(1)
    sigmoid = jax.nn.sigmoid(gate_act)
    hidden = gate_act * sigmoid * up_act
    scaled_hidden = (slot_gate * hidden).astype(low)
    out_term = jnp.einsum(
        "ecd,ecf->edf", grads_in, scaled_hidden, preferred_element_type=jnp.float32
    ).astype(low)
    out_total = lax.psum(out_term, "rep")
    hidden_grad = jnp.einsum(
        "ecd,edf->ecf", grads_in, expert_out, preferred_element_type=jnp.float32
    )
    gate_grad_slots = RESIDUAL_SCALE * jnp.sum(hidden * hidden_grad, -1)
    hidden_grad = slot_gate * hidden_grad
    gate_side = (hidden_grad * up_act * sigmoid * (1.0 + gate_act * (1.0 - sigmoid))).astype(low)
    up_side = (hidden_grad * (gate_act * sigmoid)).astype(low)
    pair_side = jnp.stack([gate_side, up_side])
    rows_grad = jnp.einsum(
        "tecf,etdf->ecd", pair_side, expert_in, preferred_element_type=jnp.float32
    ).astype(low)
    mixed = jnp.einsum(
        "ecf,edf->ecd", scaled_hidden, expert_out, preferred_element_type=jnp.float32
    ).astype(low)

    norm_grad_two, gate_grad_parts, mix = None, [], None
    for k in range(shards):
        span = slice(k * CAP, (k + 1) * CAP)
        spread = spreads[k].reshape(local * CAP, row_count)

        def collect(values):
            return jnp.einsum(
                "st,sd->td",
                spread,
                values[:, span].reshape(local * CAP, D),
                preferred_element_type=jnp.float32,
            )

        rows_part = collect(rows_grad)
        mix_part = collect(mixed)
        gate_part = jnp.sum(
            jnp.where(spreads[k] > 0, gate_grad_slots[:, span][:, :, None], 0.0), 1
        )
        if k == 0:
            norm_grad_two, mix = rows_part, mix_part
        else:
            norm_grad_two = norm_grad_two + shift(rows_part.astype(low), "shard", shards, -k)
            mix = mix + shift(mix_part.astype(low), "shard", shards, -k)
            gate_part = shift(gate_part, "shard", shards, -k)
        gate_grad_parts.append(gate_part)
    layer_out = (residual + mix).astype(low)

    in_terms = [
        jnp.einsum("ecd,ecf->edf", rows_in, part, preferred_element_type=jnp.float32).astype(low)
        for part in (gate_side, up_side)
    ]
    gate_total = lax.psum(after(in_terms[0], out_total), "rep")
    up_total = lax.psum(after(in_terms[1], gate_total), "rep")

    gate_grad = jnp.zeros((EXPERTS, row_count), jnp.float32)
    for k in range(shards):
        start = lax.rem(me + k, shards) * local
        gate_grad = lax.dynamic_update_slice_in_dim(gate_grad, gate_grad_parts[k], start, 0)
    gate_grad = gate_grad.T
    gates = home[1]
    logit_grad = gates * (gate_grad - jnp.sum(gates * gate_grad, -1, keepdims=True))
    grad_out = out_grad.astype(jnp.float32)
    exact = lax.Precision.HIGHEST
    norm_grad_two = norm_grad_two + jnp.dot(
        logit_grad, router_full.astype(jnp.float32).T, precision=exact
    )
    router_term = jnp.dot(normed_two.astype(jnp.float32).T, logit_grad, precision=exact)
    weighted_two = gain_two * norm_grad_two
    gain_two_term = jnp.sum(norm_grad_two * residual * scale_two, 0)
    residual_grad = (
        grad_out
        + scale_two * weighted_two
        - residual * scale_two**3 * jnp.mean(weighted_two * residual, -1, keepdims=True)
    )
    branch_grad = (RESIDUAL_SCALE * residual_grad).astype(low)
    output_term = jnp.einsum("tq,td->qd", attended, branch_grad, preferred_element_type=jnp.float32)
    attended_grad = jnp.einsum(
        "td,qd->tq", branch_grad, output_full, preferred_element_type=jnp.float32
    ).astype(low)
    attended_grad = attended_grad.reshape(seq_count, SEQ, KV_HEADS, group_heads, HEAD_DIM)
    scores = block_scores(queries, keys_low, 0)
    probs_f = jnp.exp(scores - log_total)
    prob_low = probs_f.astype(low)
    value_grad = jnp.einsum(
        "sgjqk,sqgjd->skgd", prob_low, attended_grad, preferred_element_type=jnp.float32
    )
    prob_grad = jnp.einsum(
        "sqgjd,skgd->sgjqk", attended_grad, value_low, preferred_element_type=jnp.float32
    )
    score_grad = (
        probs_f * (prob_grad - jnp.sum(probs_f * prob_grad, -1, keepdims=True))
    ).astype(low)
    query_grad = ATTN_SCALE * jnp.einsum(
        "sgjqk,skgd->sqgjd", score_grad, keys_low, preferred_element_type=jnp.float32
    )
    key_grad = ATTN_SCALE * jnp.einsum(
        "sgjqk,sqgjd->skgd", score_grad, queries, preferred_element_type=jnp.float32
    )
    query_low = unrotate(query_grad.reshape(seq_count, SEQ, HEADS, HEAD_DIM), cosine, sine_part)
    key_low = unrotate(key_grad, cosine, sine_part)
    qkv_low = jnp.concatenate(
        [
            query_low.reshape(row_count, query_width).astype(low),
            key_low.reshape(row_count, kv_width).astype(low),
            value_grad.reshape(row_count, kv_width).astype(low),
        ],
        1,
    )
    qkv_term = jnp.einsum("td,tq->dq", normed_one, qkv_low, preferred_element_type=jnp.float32)
    norm_grad_one = jnp.einsum(
        "tq,dq->td", qkv_low, qkv_full, preferred_element_type=jnp.float32
    )
    weighted_one = gain_one * norm_grad_one
    gain_one_term = jnp.sum(norm_grad_one * inputs_f * scale_one, 0)
    tokens_grad = (
        residual_grad
        + scale_one * weighted_one
        - inputs_f * scale_one**3 * jnp.mean(weighted_one * inputs_f, -1, keepdims=True)
    )
    small = jnp.concatenate(
        [
            qkv_term.astype(low),
            output_term.astype(low),
            router_term.astype(low),
            gain_one_term[:, None].astype(low),
            gain_two_term[:, None].astype(low),
            jnp.zeros((D, 128 - EXPERTS - 2), low),
        ],
        1,
    )
    own = D // shards

    def rows_for(step):
        return lax.dynamic_slice_in_dim(small, lax.rem(me + step, shards) * own, own, 0)

    share = rows_for(0).astype(jnp.float32)
    for k in range(1, shards):
        share = share + shift(rows_for(k), "shard", shards, k)
    share = after(share.astype(low), up_total)
    total = lax.psum(share, "rep").astype(jnp.float32)
    base = query_width + 2 * kv_width
    side = total[:, base + D :]
    return (
        layer_out,
        tokens_grad,
        total[:, :query_width],
        total[:, query_width : query_width + kv_width],
        total[:, query_width + kv_width : base],
        total[:, base : base + D],
        side[:, EXPERTS],
        side[:, EXPERTS + 1],
        side[:, :EXPERTS],
        jnp.stack([gate_total, up_total], 1).astype(jnp.float32),
        out_total.astype(jnp.float32),
    )


def solution(mesh):
    return jax.shard_map(
        functools.partial(per_device, mesh.shape["shard"], mesh.shape["rep"]),
        mesh=mesh,
        in_specs=(
            P(("shard", "rep"), None),
            P(("shard", "rep"), None),
            P(("shard", "rep"), None),
            P("shard", None),
            P("shard", None),
            P("shard", None),
            P("shard", None),
            P("shard"),
            P("shard"),
            P("shard", None),
            P("shard", None, None, None),
            P("shard", None, None),
        ),
        out_specs=(
            P(("shard", "rep"), None),
            P(("shard", "rep"), None),
            P("shard", None),
            P("shard", None),
            P("shard", None),
            P("shard", None),
            P("shard"),
            P("shard"),
            P("shard", None),
            P("shard", None, None, None),
            P("shard", None, None),
        ),
        check_vma=False,
    )
```

```python
import functools

import jax
import jax.numpy as jnp
from jax import lax
from jax.sharding import PartitionSpec as P

D = 1024
HEADS = 16
KV_HEADS = 8
HEAD_DIM = 64
EXPERTS = 16
SEQ = 512
CAP = 288


EPSILON = 1e-06
ATTN_SCALE = 0.015625
RESIDUAL_SCALE = 0.22
ROPE_BASE = 10000.0


def rope_tables(length, width):
    half_width = width // 2
    frequency = ROPE_BASE ** (-2.0 * jnp.arange(half_width, dtype=jnp.float32) / width)
    angles = jnp.arange(length, dtype=jnp.float32)[:, None] * frequency[None, :]
    return (jnp.cos(angles)[:, None, :], jnp.sin(angles)[:, None, :])


def rotate(values, cosine, sine_part):
    half_width = values.shape[-1] // 2
    first_half = values[..., :half_width]
    second_half = values[..., half_width:]
    return jnp.concatenate(
        [
            first_half * cosine - second_half * sine_part,
            second_half * cosine + first_half * sine_part,
        ],
        -1,
    )


def unrotate(values, cosine, sine_part):
    half_width = values.shape[-1] // 2
    first_half = values[..., :half_width]
    second_half = values[..., half_width:]
    return jnp.concatenate(
        [
            first_half * cosine + second_half * sine_part,
            second_half * cosine - first_half * sine_part,
        ],
        -1,
    )


def block_scores(query_block, key_block, first_row):
    scores = ATTN_SCALE * jnp.einsum(
        "sqgjd,skgd->sgjqk", query_block, key_block, preferred_element_type=jnp.float32
    )
    query_pos = first_row + jnp.arange(query_block.shape[1])
    key_pos = jnp.arange(key_block.shape[1])
    return jnp.where(query_pos[:, None] >= key_pos[None, :], scores, -jnp.inf)


def shift(value, axis, size, step):
    return lax.ppermute(value, axis, [(i, (i + step) % size) for i in range(size)])


def after(value, *others):
    return lax.optimization_barrier((value,) + others)[0]


def gather_rows(block, shards, reps):
    me = lax.axis_index("shard")
    odd = lax.rem(lax.axis_index("rep"), 2)
    rows, width = block.shape
    half = rows // 2
    mine = lax.dynamic_slice_in_dim(block, odd * half, half, 0)
    swap = [(i, i ^ 1) for i in range(reps)]
    whole = jnp.zeros((shards * rows, width), block.dtype)
    whole = lax.dynamic_update_slice_in_dim(whole, block, me * rows, 0)
    for step in range(1, shards):
        owner = lax.rem(me - step + shards, shards)
        first = shift(mine, "shard", shards, step)
        second = lax.ppermute(first, "rep", swap)
        whole = lax.dynamic_update_slice_in_dim(whole, first, owner * rows + odd * half, 0)
        whole = lax.dynamic_update_slice_in_dim(whole, second, owner * rows + (1 - odd) * half, 0)
    return whole


def flip(value, size, bit):
    return lax.ppermute(value, "rep", [(i, i ^ (1 << bit)) for i in range(size)])


def halve(block, reps, bit):
    half = block.shape[0] // 2
    odd = (lax.axis_index("rep") >> bit) & 1
    given = lax.dynamic_slice_in_dim(block, (1 - odd) * half, half, 0)
    kept = lax.dynamic_slice_in_dim(block, odd * half, half, 0)
    taken = flip(given, reps, bit)
    return (kept.astype(jnp.float32) + taken.astype(jnp.float32)).astype(block.dtype)


def ordered(block, taken, bit, kind):
    odd = (lax.axis_index("rep") >> bit) & 1
    half = block.shape[0]
    whole = jnp.zeros((2 * half,) + block.shape[1:], kind)
    whole = lax.dynamic_update_slice_in_dim(whole, block.astype(kind), odd * half, 0)
    return lax.dynamic_update_slice_in_dim(whole, taken.astype(kind), (1 - odd) * half, 0)


def double(block, reps, bit):
    return ordered(block, flip(block, reps, bit), bit, block.dtype)


def per_device(
    shards,
    reps,
    tokens,
    routes,
    out_grad,
    query_weight,
    key_weight,
    value_weight,
    output_weight,
    norm_one,
    norm_two,
    router_weight,
    expert_in,
    expert_out,
):
    row_count = tokens.shape[0]
    seq_count = row_count // SEQ
    group_heads = HEADS // KV_HEADS
    query_width = HEADS * HEAD_DIM
    kv_width = KV_HEADS * HEAD_DIM
    local = EXPERTS // shards
    low = jnp.bfloat16
    me = lax.axis_index("shard")
    side = jnp.concatenate(
        [router_weight, norm_one[:, None], norm_two[:, None]]
        + [jnp.zeros((router_weight.shape[0], 128 - EXPERTS - 2), low)],
        1,
    )
    first_full = gather_rows(
        jnp.concatenate([query_weight, key_weight, value_weight, side], 1), shards, reps
    )
    output_full = gather_rows(after(output_weight, first_full), shards, reps)
    qkv_full = first_full[:, : query_width + 2 * kv_width]
    query_full = first_full[:, :query_width]
    key_full = first_full[:, query_width : query_width + kv_width]
    value_full = first_full[:, query_width + kv_width : query_width + 2 * kv_width]
    base = query_width + 2 * kv_width
    router_full = first_full[:, base : base + EXPERTS]
    gain_one = first_full[:, base + EXPERTS].astype(jnp.float32)
    gain_two = first_full[:, base + EXPERTS + 1].astype(jnp.float32)
    grad_send = after(out_grad, output_full)
    grad_groups = [out_grad] + [shift(grad_send, "shard", shards, k) for k in range(1, shards)]
    route_groups = [routes] + [shift(routes, "shard", shards, k) for k in range(1, shards)]

    inputs_f = tokens.astype(jnp.float32)
    scale_one = lax.rsqrt(jnp.mean(inputs_f * inputs_f, -1, keepdims=True) + EPSILON)
    normed_one = (inputs_f * scale_one * gain_one).astype(low)
    query_pre = jnp.dot(normed_one, query_full, preferred_element_type=jnp.float32)
    key_pre = jnp.dot(normed_one, key_full, preferred_element_type=jnp.float32)
    value_low = jnp.dot(normed_one, value_full, preferred_element_type=jnp.float32).astype(low)
    value_low = value_low.reshape(seq_count, SEQ, KV_HEADS, HEAD_DIM)
    cosine, sine_part = rope_tables(SEQ, HEAD_DIM)
    queries = rotate(query_pre.reshape(seq_count, SEQ, HEADS, HEAD_DIM), cosine, sine_part).astype(
        low
    )
    queries = queries.reshape(seq_count, SEQ, KV_HEADS, group_heads, HEAD_DIM)
    keys_low = rotate(
        key_pre.reshape(seq_count, SEQ, KV_HEADS, HEAD_DIM), cosine, sine_part
    ).astype(low)
    scores = block_scores(queries, keys_low, 0)
    row_max = jnp.max(scores, -1, keepdims=True)
    exp_scores = jnp.exp(scores - row_max)
    row_total = jnp.sum(exp_scores, -1, keepdims=True)
    prob_low = (exp_scores / row_total).astype(low)
    head_outputs = jnp.einsum(
        "sgjqk,skgd->sqgjd", prob_low, value_low, preferred_element_type=jnp.float32
    )
    log_total = row_max + jnp.log(row_total)
    attended = head_outputs.reshape(row_count, query_width).astype(low)
    branch = jnp.dot(attended, output_full, preferred_element_type=jnp.float32)
    residual = inputs_f + RESIDUAL_SCALE * branch
    scale_two = lax.rsqrt(jnp.mean(residual * residual, -1, keepdims=True) + EPSILON)
    normed_two = (residual * scale_two * gain_two).astype(low)

    group_rows = [normed_two] + [shift(normed_two, "shard", shards, k) for k in range(1, shards)]
    experts_iota = jnp.arange(EXPERTS, dtype=jnp.int32)
    triangle = (jnp.arange(row_count)[:, None] > jnp.arange(row_count)[None, :]).astype(low)

    def gates_of(rows, group_routes):
        named = jnp.any(group_routes[:, :, None] == experts_iota, 1)
        logits = jnp.dot(rows, router_full, preferred_element_type=jnp.float32)
        return named, jax.nn.softmax(jnp.where(named, logits, -jnp.inf), -1)

    def mine_of(table):
        return lax.dynamic_slice_in_dim(table, me * local, local, 1)

    spreads, rows_slots, grad_slots, gate_slots = [], [], [], []
    slots = jnp.arange(CAP, dtype=jnp.int32)
    home = None
    for k in range(shards):
        named, gates = gates_of(group_rows[k], route_groups[k])
        if k == 0:
            home = (named, gates)
        ranks = jnp.dot(triangle, named.astype(low), preferred_element_type=jnp.float32)
        ranks = jnp.where(named, ranks.astype(jnp.int32), -1)
        place = mine_of(ranks).T
        hit = place[:, None, :] == slots[None, :, None]
        spread = hit.astype(low)
        spreads.append(spread)
        flat = spread.reshape(local * CAP, row_count)
        rows_slots.append(
            jnp.dot(flat, group_rows[k], preferred_element_type=jnp.float32)
            .astype(low)
            .reshape(local, CAP, D)
        )
        grad_slots.append(
            jnp.dot(flat, grad_groups[k], preferred_element_type=jnp.float32)
            .astype(low)
            .reshape(local, CAP, D)
        )
        gate_slots.append(jnp.sum(jnp.where(hit, mine_of(gates).T[:, None, :], 0.0), -1))
    rows_in = jnp.concatenate(rows_slots, 1)
    grads_in = jnp.concatenate(grad_slots, 1)
    slot_gate = jnp.concatenate(gate_slots, 1)[:, :, None] * RESIDUAL_SCALE

    bits = reps.bit_length() - 1

    def step_down(block, bit):
        return halve(block, reps, bit) if bit < bits else block

    def step_up(block, bit):
        return double(block, reps, bit) if bit < bits else block

    def up(part):
        return jnp.einsum(
            "ecd,edf->ecf", rows_in, expert_in[:, part], preferred_element_type=jnp.float32
        )

    gate_act, up_act = up(0), up(1)
    sigmoid = jax.nn.sigmoid(gate_act)
    hidden = gate_act * sigmoid * up_act
    scaled_hidden = (slot_gate * hidden).astype(low)
    out_term = jnp.einsum(
        "ecd,ecf->edf", grads_in, scaled_hidden, preferred_element_type=jnp.float32
    ).astype(low)
    out_sum = halve(out_term.reshape(-1, out_term.shape[-1]), reps, 0)
    hidden_grad = jnp.einsum(
        "ecd,edf->ecf", after(grads_in, out_term), expert_out, preferred_element_type=jnp.float32
    )
    gate_grad_slots = RESIDUAL_SCALE * jnp.sum(hidden * hidden_grad, -1)
    hidden_grad = slot_gate * hidden_grad
    gate_side = (hidden_grad * up_act * sigmoid * (1.0 + gate_act * (1.0 - sigmoid))).astype(low)
    up_side = (hidden_grad * (gate_act * sigmoid)).astype(low)
    gate_side, up_side, out_sum = lax.optimization_barrier((gate_side, up_side, out_sum))
    out_sum = step_down(out_sum, 1)
    in_terms = [
        jnp.einsum("ecd,ecf->edf", rows_in, part, preferred_element_type=jnp.float32).astype(low)
        for part in (gate_side, up_side)
    ]
    gate_later, up_later, out_sum, gate_term, up_term = lax.optimization_barrier(
        (gate_side, up_side, out_sum, in_terms[0], in_terms[1])
    )
    gate_sum = halve(gate_term.reshape(-1, gate_term.shape[-1]), reps, 0)
    up_sum = halve(up_term.reshape(-1, up_term.shape[-1]), reps, 0)
    out_sum = step_down(out_sum, 2)
    pair_side = jnp.stack([gate_later, up_later])
    rows_grad = jnp.einsum(
        "tecf,etdf->ecd", pair_side, expert_in, preferred_element_type=jnp.float32
    ).astype(low)
    rows_grad, gate_sum, up_sum, out_sum = lax.optimization_barrier(
        (rows_grad, gate_sum, up_sum, out_sum)
    )
    gate_sum, out_sum = step_down(gate_sum, 1), step_down(out_sum, 3)
    for bit in range(4, bits):
        out_sum = halve(out_sum, reps, bit)
    up_sum = step_down(up_sum, 1)
    mixed = jnp.einsum(
        "ecf,edf->ecd", scaled_hidden, expert_out, preferred_element_type=jnp.float32
    ).astype(low)

    norm_grad_two, gate_grad_parts, mix = None, [], None
    for k in range(shards):
        span = slice(k * CAP, (k + 1) * CAP)
        spread = spreads[k].reshape(local * CAP, row_count)

        def collect(values):
            return jnp.einsum(
                "st,sd->td",
                spread,
                values[:, span].reshape(local * CAP, D),
                preferred_element_type=jnp.float32,
            )

        rows_part = collect(rows_grad)
        mix_part = collect(mixed)
        gate_part = jnp.sum(
            jnp.where(spreads[k] > 0, gate_grad_slots[:, span][:, :, None], 0.0), 1
        )
        if k == 0:
            norm_grad_two, mix = rows_part, mix_part
        else:
            norm_grad_two = norm_grad_two + shift(rows_part.astype(low), "shard", shards, -k)
            mix = mix + shift(mix_part.astype(low), "shard", shards, -k)
            gate_part = shift(gate_part, "shard", shards, -k)
        gate_grad_parts.append(gate_part)
    layer_out = (residual + mix).astype(low)

    gate_grad = jnp.zeros((EXPERTS, row_count), jnp.float32)
    for k in range(shards):
        start = lax.rem(me + k, shards) * local
        gate_grad = lax.dynamic_update_slice_in_dim(gate_grad, gate_grad_parts[k], start, 0)
    gate_grad = gate_grad.T
    gates = home[1]
    logit_grad = gates * (gate_grad - jnp.sum(gates * gate_grad, -1, keepdims=True))
    grad_out = out_grad.astype(jnp.float32)
    exact = lax.Precision.HIGHEST
    norm_grad_two = norm_grad_two + jnp.dot(
        logit_grad, router_full.astype(jnp.float32).T, precision=exact
    )
    router_term = jnp.dot(normed_two.astype(jnp.float32).T, logit_grad, precision=exact)
    norm_grad_two, gate_sum, out_sum = lax.optimization_barrier((norm_grad_two, gate_sum, out_sum))
    for bit in reversed(range(3, bits)):
        out_sum = double(out_sum, reps, bit)
    gate_sum = step_down(gate_sum, 2)
    weighted_two = gain_two * norm_grad_two
    gain_two_term = jnp.sum(norm_grad_two * residual * scale_two, 0)
    residual_grad = (
        grad_out
        + scale_two * weighted_two
        - residual * scale_two**3 * jnp.mean(weighted_two * residual, -1, keepdims=True)
    )
    branch_grad = (RESIDUAL_SCALE * residual_grad).astype(low)
    output_term = jnp.einsum("tq,td->qd", attended, branch_grad, preferred_element_type=jnp.float32)
    attended_grad = jnp.einsum(
        "td,qd->tq", branch_grad, output_full, preferred_element_type=jnp.float32
    ).astype(low)
    attended_grad = attended_grad.reshape(seq_count, SEQ, KV_HEADS, group_heads, HEAD_DIM)
    scores = block_scores(queries, keys_low, 0)
    probs_f = jnp.exp(scores - log_total)
    prob_low = probs_f.astype(low)
    value_grad = jnp.einsum(
        "sgjqk,sqgjd->skgd", prob_low, attended_grad, preferred_element_type=jnp.float32
    )
    prob_grad = jnp.einsum(
        "sqgjd,skgd->sgjqk", attended_grad, value_low, preferred_element_type=jnp.float32
    )
    score_grad = (
        probs_f * (prob_grad - jnp.sum(probs_f * prob_grad, -1, keepdims=True))
    ).astype(low)
    score_grad, up_sum, gate_sum, out_sum = lax.optimization_barrier(
        (score_grad, up_sum, gate_sum, out_sum)
    )
    out_sum, up_sum = step_up(out_sum, 2), step_down(up_sum, 2)
    for bit in range(3, bits):
        gate_sum = halve(gate_sum, reps, bit)
    query_grad = ATTN_SCALE * jnp.einsum(
        "sgjqk,skgd->sqgjd", score_grad, keys_low, preferred_element_type=jnp.float32
    )
    key_grad = ATTN_SCALE * jnp.einsum(
        "sgjqk,sqgjd->skgd", score_grad, queries, preferred_element_type=jnp.float32
    )
    query_low = unrotate(query_grad.reshape(seq_count, SEQ, HEADS, HEAD_DIM), cosine, sine_part)
    key_low = unrotate(key_grad, cosine, sine_part)
    qkv_low = jnp.concatenate(
        [
            query_low.reshape(row_count, query_width).astype(low),
            key_low.reshape(row_count, kv_width).astype(low),
            value_grad.reshape(row_count, kv_width).astype(low),
        ],
        1,
    )
    qkv_low, gate_sum, up_sum, out_sum = lax.optimization_barrier(
        (qkv_low, gate_sum, up_sum, out_sum)
    )
    out_sum = step_up(out_sum, 1)
    for bit in range(3, bits):
        up_sum = halve(up_sum, reps, bit)
    for bit in reversed(range(2, bits)):
        gate_sum = double(gate_sum, reps, bit)
    qkv_term = jnp.einsum("td,tq->dq", normed_one, qkv_low, preferred_element_type=jnp.float32)
    norm_grad_one = jnp.einsum(
        "tq,dq->td", qkv_low, qkv_full, preferred_element_type=jnp.float32
    )
    weighted_one = gain_one * norm_grad_one
    gain_one_term = jnp.sum(norm_grad_one * inputs_f * scale_one, 0)
    tokens_grad = (
        residual_grad
        + scale_one * weighted_one
        - inputs_f * scale_one**3 * jnp.mean(weighted_one * inputs_f, -1, keepdims=True)
    )
    small = jnp.concatenate(
        [
            qkv_term.astype(low),
            output_term.astype(low),
            router_term.astype(low),
            gain_one_term[:, None].astype(low),
            gain_two_term[:, None].astype(low),
            jnp.zeros((D, 128 - EXPERTS - 2), low),
        ],
        1,
    )
    own = D // shards

    def rows_for(step):
        return lax.dynamic_slice_in_dim(small, lax.rem(me + step, shards) * own, own, 0)

    share = rows_for(0).astype(jnp.float32)
    for k in range(1, shards):
        share = share + shift(rows_for(k), "shard", shards, k)
    share = share.astype(low)
    for bit in range(bits):
        share = halve(share, reps, bit)
    for bit in reversed(range(bits)):
        share = double(share, reps, bit)
    total = share.astype(jnp.float32)
    for bit in reversed(range(2, bits)):
        up_sum = double(up_sum, reps, bit)
    gate_sum, up_sum = step_up(gate_sum, 1), step_up(up_sum, 1)

    def blocks(value):
        return value.reshape(-1, D, value.shape[-1])

    odd = lax.rem(lax.axis_index("rep"), 2)
    in_total = jnp.zeros((local, 2, D, gate_sum.shape[-1]), jnp.float32)
    for part, value in enumerate((gate_sum, up_sum)):
        for place, piece in ((odd, value), (1 - odd, flip(value, reps, 0))):
            in_total = lax.dynamic_update_slice(
                in_total,
                blocks(piece)[:, None].astype(jnp.float32),
                (place * (local // 2), part, 0, 0),
            )
    out_total = blocks(ordered(out_sum, flip(out_sum, reps, 0), 0, jnp.float32))
    base = query_width + 2 * kv_width
    side = total[:, base + D :]
    return (
        layer_out,
        tokens_grad,
        total[:, :query_width],
        total[:, query_width : query_width + kv_width],
        total[:, query_width + kv_width : base],
        total[:, base : base + D],
        side[:, EXPERTS],
        side[:, EXPERTS + 1],
        side[:, :EXPERTS],
        in_total,
        out_total,
    )


def solution(mesh):
    return jax.shard_map(
        functools.partial(per_device, mesh.shape["shard"], mesh.shape["rep"]),
        mesh=mesh,
        in_specs=(
            P(("shard", "rep"), None),
            P(("shard", "rep"), None),
            P(("shard", "rep"), None),
            P("shard", None),
            P("shard", None),
            P("shard", None),
            P("shard", None),
            P("shard"),
            P("shard"),
            P("shard", None),
            P("shard", None, None, None),
            P("shard", None, None),
        ),
        out_specs=(
            P(("shard", "rep"), None),
            P(("shard", "rep"), None),
            P("shard", None),
            P("shard", None),
            P("shard", None),
            P("shard", None),
            P("shard"),
            P("shard"),
            P("shard", None),
            P("shard", None, None, None),
            P("shard", None, None),
        ),
        check_vma=False,
    )
```
